1024 devices in a mesh: owner: 64 (over z, x), red: 8 (over y), rep: 2 (over core).
Axes of the slice: x: 8, y: 8, z: 8, core: 2. Of those that a mesh axis runs over, the one named last changes fastest.
Arguments:
- amps: bfloat16 [1024, 16384], P('owner', ('red', 'rep')), may hold values from -6 to 6
- integrals: bfloat16 [16384, 65536], P(('red', 'rep'), 'owner'), may hold values from -0.15625 to 0.15625
- shape: int32 [128, 512], P(('red', 'rep'), 'owner'), may hold values from 0 to 1, as said below
Outputs:
- residual: bfloat16 [1024, 65536], P(('red', 'rep'), 'owner')
The draws below stay inside these ranges and needn't reach their ends.
Inputs may be any that keep to these rules, and one draw needn't show every extreme that they name: shape[q, p] is 1 where amplitude tile q and residual tile p are coupled, else 0; the integral blocks are given dense and the bitmap selects which enter.
All inputs are finite; a program needn't handle non-finite values.
Results may differ from the reference program's by a relative error of at most 0.018.
Values may be sent and summed in bfloat16 or wider, within the bound.
No kernel may reach another device: no remote copies, remote signals or barrier semaphores. Data moves between devices by JAX's collectives and lax.ppermute only.
A program may use at most 32 MiB of HBM per device.

```python
import jax
import jax.numpy as jnp
from jax import lax

TILE = 128
QDEV = 8
PDEV = 8
ROWS = 1024
NQ = 128
NP = 512


def draw_shape(key, part):
    key = jax.random.fold_in(key, 7)
    level_key, roll_key = jax.random.split(key)
    levels = jax.random.randint(level_key, (NP // PDEV,), 1, 10)
    cutoff = jnp.repeat(levels, PDEV)
    rolled = jax.random.randint(roll_key, (NQ, NP), 0, 64)
    return (rolled < cutoff[None, :]).astype(jnp.int32)


def steps_of(stream_key, shape, cuts, low, top_value):
    loudness, own = 1.0, jax.random.fold_in(stream_key, 6)
    for dim, blocks in cuts:
        draws = jnp.exp(jax.random.uniform(jax.random.fold_in(own, dim), (blocks,), jnp.float32, low / len(cuts), top_value / len(cuts)))
        loudness = loudness * jnp.repeat(draws, shape[dim] // blocks).reshape([-1 if axis == dim else 1 for axis in range(len(shape))])
    return loudness


def noise(key, shape, scale, reach, shards=(), kind=jnp.bfloat16):
    values = jax.random.normal(key, shape, jnp.float32) * scale
    if len(shards) > 0:
        values = steps_of(key, shape, shards, -0.22, 0.18) * values
    return jnp.clip(values, min=-reach, max=reach).astype(kind)


def setup_inputs(seed: int = 0) -> dict:
    arg_keys = jax.random.split(jax.random.key(seed), 4)
    return {
        "amps": noise(arg_keys[0], (ROWS, NQ * TILE), 1.0, 6.0, ((0, 64), (1, 16))),
        "integrals": noise(arg_keys[1], (NQ * TILE, NP * TILE), (NQ * TILE * 5 // 64) ** -0.5, 0.15625, ((0, 16), (1, 64))),
        "shape": draw_shape(jax.random.fold_in(arg_keys[3], 71), 0),
    }


def reference(amps, integrals, shape):
    blocks = NP // PDEV
    groups = NQ // QDEV
    width = QDEV * TILE
    amp_groups = jnp.transpose(amps.reshape(ROWS, groups, width), (1, 0, 2))

    def one_owner(block_index):
        column_block = lax.dynamic_slice_in_dim(integrals, block_index * (PDEV * TILE), PDEV * TILE, 1)
        block_bits = lax.dynamic_slice_in_dim(shape, block_index * PDEV, PDEV, 1).astype(jnp.bfloat16)
        masked = (column_block.reshape(NQ, TILE, PDEV, TILE) * block_bits[:, None, :, None]).reshape(groups, width, PDEV * TILE)

        def add_group(total, index):
            term = jnp.dot(amp_groups[index], masked[index], preferred_element_type=jnp.float32)
            return total + term.astype(jnp.bfloat16).astype(jnp.float32), None

        start = jnp.zeros((ROWS, PDEV * TILE), jnp.float32)
        total, unused = lax.scan(add_group, start, jnp.arange(groups, dtype=jnp.int32))
        return total.astype(jnp.bfloat16)

    stacked = lax.map(one_owner, jnp.arange(blocks, dtype=jnp.int32))
    return jnp.transpose(stacked, (1, 0, 2)).reshape(ROWS, NP * TILE)
```

```python
import functools

import jax
import jax.numpy as jnp
from jax import lax
from jax.experimental import pallas as pl
from jax.experimental.pallas import tpu as pltpu
from jax.sharding import PartitionSpec as P

TILE = 128
SIDE = 8
ROWS = 16


def line_groups(first_phase):
    along_x, along_z = (0, 1) if first_phase else (1, 0)
    groups = [[(z * SIDE + x) * 2 + along_x for x in range(SIDE)] for z in range(SIDE)]
    groups += [[(z * SIDE + x) * 2 + along_z for z in range(SIDE)] for x in range(SIDE)]
    return groups


def spread(block, groups):
    copies = jnp.broadcast_to(block[None], (SIDE,) + block.shape)
    return lax.all_to_all(copies, ("owner", "rep"), 0, 0, axis_index_groups=groups, tiled=True)


def masked_dot_kernel(other, rep_ref, bits_ref, amps_ref, ints_ref, out_ref, masked_ref):
    step = pl.program_id(0)
    col_tiles = ints_ref.shape[1] // TILE
    for q in range(ints_ref.shape[0] // TILE):
        for p in range(col_tiles):
            here = (slice(q * TILE, (q + 1) * TILE), slice(p * TILE, (p + 1) * TILE))
            bit = bits_ref[q, step * col_tiles + p].astype(jnp.float32)
            masked_ref[here] = ints_ref[here] * bit.astype(ints_ref.dtype)
    rep = rep_ref[0]
    half = SIDE // 2
    depth = amps_ref.shape[-1]

    @pl.when(rep == 0)
    def _():
        low = half if other else 0
        rows = amps_ref[:, low : low + half].reshape(SIDE * half * ROWS, depth)
        total = jnp.dot(rows, masked_ref[...], preferred_element_type=jnp.float32)
        out_ref[...] = total.astype(out_ref.dtype).reshape(out_ref.shape)

    @pl.when(rep == 1)
    def _():
        low = 0 if other else half
        rows = amps_ref[low : low + half].reshape(half * SIDE * ROWS, depth)
        total = jnp.dot(rows, masked_ref[...], preferred_element_type=jnp.float32)
        total = total.astype(out_ref.dtype).reshape((half, SIDE, ROWS, total.shape[-1]))
        for x in range(half):
            out_ref[:, x] = total[x]


def masked_dot(other, rep, bits, gathered, ints):
    depth, cols = ints.shape
    width = 256
    half = SIDE // 2
    return pl.pallas_call(
        functools.partial(masked_dot_kernel, other),
        grid=(cols // width,),
        in_specs=[
            pl.BlockSpec(memory_space=pltpu.SMEM),
            pl.BlockSpec(memory_space=pltpu.SMEM),
            pl.BlockSpec(gathered.shape, lambda i: (0, 0, 0, 0)),
            pl.BlockSpec((depth, width), lambda i: (0, i)),
        ],
        out_specs=pl.BlockSpec((SIDE, half, ROWS, width), lambda i: (0, 0, 0, i)),
        out_shape=jax.ShapeDtypeStruct((SIDE, half, ROWS, cols), jnp.bfloat16),
        scratch_shapes=[pltpu.VMEM((depth, width), jnp.bfloat16)],
        compiler_params=pltpu.CompilerParams(vmem_limit_bytes=32 * 1024 * 1024),
        cost_estimate=pl.CostEstimate(
            flops=SIDE * half * ROWS * depth * cols * 2, bytes_accessed=5 * 1024 * 1024, transcendentals=0
        ),
    )(rep, bits, gathered, ints)


def per_device(amps, ints, bits):
    rep = lax.axis_index("rep").astype(jnp.int32).reshape(1)
    line = spread(amps, line_groups(True))
    plane = spread(line, line_groups(False))
    plane = plane.reshape(SIDE, SIDE, ROWS, amps.shape[1])
    away = masked_dot(True, rep, bits, plane, ints)
    arrived = lax.ppermute(away, "rep", [(0, 1), (1, 0)])
    kept = masked_dot(False, rep, bits, plane, ints)
    both = (kept.astype(jnp.float32) + arrived.astype(jnp.float32)).astype(jnp.bfloat16)
    shares = lax.all_to_all(both.reshape(SIDE, -1, ints.shape[1]), "red", 0, 0, tiled=True)
    return jnp.sum(shares.astype(jnp.float32), axis=0).astype(jnp.bfloat16)


def solution(mesh):
    return jax.shard_map(
        per_device,
        mesh=mesh,
        in_specs=(
            P("owner", ("red", "rep")),
            P(("red", "rep"), "owner"),
            P(("red", "rep"), "owner"),
        ),
        out_specs=P(("red", "rep"), "owner"),
        check_vma=False,
    )
```

```python
import functools

import jax
import jax.numpy as jnp
from jax import lax
from jax.experimental import pallas as pl
from jax.experimental.pallas import tpu as pltpu
from jax.sharding import PartitionSpec as P

TILE = 128
SIDE = 8
HALF = SIDE // 2
ROWS = 16
VMEM = pl.BlockSpec(memory_space=pltpu.VMEM)
SMEM = pl.BlockSpec(memory_space=pltpu.SMEM)


def line_groups():
    groups = [[(z * SIDE + x) * 2 for x in range(SIDE)] for z in range(SIDE)]
    groups += [[(z * SIDE + x) * 2 + 1 for z in range(SIDE)] for x in range(SIDE)]
    return groups


def ring_step(step):
    pairs = []
    for z in range(SIDE):
        for x in range(SIDE):
            here = (z * SIDE + x) * 2
            pairs.append((here, ((z + step) % SIDE * SIDE + x) * 2))
            pairs.append((here + 1, (z * SIDE + (x + step) % SIDE) * 2 + 1))
    return pairs


def red_step(step):
    return [(y * 2 + c, (y + (step if c == 0 else -step)) % SIDE * 2 + c) for y in range(SIDE) for c in range(2)]


def mask_kernel(bits_ref, ints_ref, out_ref):
    for q in range(ints_ref.shape[0] // TILE):
        for p in range(ints_ref.shape[1] // TILE):
            here = (slice(q * TILE, (q + 1) * TILE), slice(p * TILE, (p + 1) * TILE))
            bit = bits_ref[q, p].astype(jnp.float32).astype(ints_ref.dtype)
            out_ref[here] = ints_ref[here] * bit


def mask(bits, ints):
    return pl.pallas_call(
        mask_kernel,
        in_specs=[SMEM, VMEM],
        out_specs=VMEM,
        out_shape=jax.ShapeDtypeStruct(ints.shape, ints.dtype),
        compiler_params=pltpu.CompilerParams(vmem_limit_bytes=16 * 1024 * 1024),
        cost_estimate=pl.CostEstimate(flops=ints.size, bytes_accessed=4 * ints.size, transcendentals=0),
    )(bits, ints)


def planes_kernel(steps, place_ref, *refs):
    count = len(steps)
    planes, masked_ref = refs[:count], refs[count]
    kept_ref, away_ref = refs[-2:]
    depth, cols = masked_ref.shape
    rep = place_ref[0]
    width = 256
    rows = jnp.concatenate([plane[...].reshape(SIDE * ROWS, depth) for plane in planes], axis=0)
    for start in range(0, cols, width):
        here = slice(start, start + width)
        total = jnp.dot(rows, masked_ref[:, here], preferred_element_type=jnp.float32)
        total = total.astype(kept_ref.dtype).reshape(count, SIDE, ROWS, width)
        for i in range(count):
            index = (place_ref[1] + (steps[i] + SIDE)) & (SIDE - 1)

            @pl.when(rep == 0)
            def _(i=i, index=index):
                kept_ref[index, :, :, here] = total[i, :HALF]
                away_ref[index, :, :, here] = total[i, HALF:]

            @pl.when((rep == 1) & (index < HALF))
            def _(i=i, index=index):
                away_ref[:, index, :, here] = total[i]

            @pl.when((rep == 1) & (index >= HALF))
            def _(i=i, index=index):
                kept_ref[:, index - HALF, :, here] = total[i]


def planes_dot(place, steps, planes, masked, sums):
    count = len(planes)
    depth, cols = masked.shape
    shape = jax.ShapeDtypeStruct((SIDE, HALF, ROWS, cols), jnp.bfloat16)
    operands = [place, *planes, masked, *sums]
    aliases = {2 + count + i: i for i in range(len(sums))}
    return pl.pallas_call(
        functools.partial(planes_kernel, steps),
        in_specs=[SMEM] + [VMEM] * (len(operands) - 1),
        out_specs=[VMEM, VMEM],
        out_shape=[shape, shape],
        input_output_aliases=aliases,
        compiler_params=pltpu.CompilerParams(vmem_limit_bytes=16 * 1024 * 1024),
        cost_estimate=pl.CostEstimate(
            flops=count * SIDE * ROWS * depth * cols * 2, bytes_accessed=1024 * 1024, transcendentals=0
        ),
    )(*operands)


def share_kernel(place_ref, kept_ref, arrived_ref, near_a_ref, near_b_ref, own_ref):
    y, way = place_ref[2], 1 - 2 * place_ref[0]

    def block(index):
        index = (index + SIDE) & (SIDE - 1)
        both = kept_ref[index].astype(jnp.float32) + arrived_ref[index].astype(jnp.float32)
        return both.astype(own_ref.dtype).reshape(HALF * ROWS, both.shape[-1])

    there = y + way
    near_a_ref[0] = block(there + 4)
    near_a_ref[1] = block(there - 2 * way)
    near_b_ref[0] = block(there + 2 * way)
    near_b_ref[1] = block(there)
    own_ref[0] = block(y + 4)
    own_ref[1] = block(y - 2 * way)
    own_ref[2] = block(y + 2 * way)
    own_ref[3] = block(y)


def share(place, kept, arrived):
    cols = kept.shape[-1]
    pair = jax.ShapeDtypeStruct((2, HALF * ROWS, cols), kept.dtype)
    four = jax.ShapeDtypeStruct((4, HALF * ROWS, cols), kept.dtype)
    return pl.pallas_call(
        share_kernel,
        in_specs=[SMEM, VMEM, VMEM],
        out_specs=[VMEM, VMEM, VMEM],
        out_shape=[pair, pair, four],
        compiler_params=pltpu.CompilerParams(vmem_limit_bytes=16 * 1024 * 1024),
        cost_estimate=pl.CostEstimate(flops=kept.size, bytes_accessed=6 * kept.size, transcendentals=0),
    )(place, kept, arrived)


def added(*terms):
    return sum(t.astype(jnp.float32) for t in terms).astype(jnp.bfloat16)


def per_device(amps, ints, bits):
    owner, y, rep = (lax.axis_index(name).astype(jnp.int32) for name in ("owner", "red", "rep"))
    z, x = owner >> 3, owner & (SIDE - 1)
    place = jnp.stack([rep, jnp.where(rep == 0, z, x), y])

    copies = jnp.broadcast_to(amps[None], (SIDE,) + amps.shape)
    line = lax.all_to_all(copies, ("owner", "rep"), 0, 0, axis_index_groups=line_groups(), tiled=True)
    masked = mask(bits, ints)

    sums = ()
    from_low, from_high = line, line
    sums = planes_dot(place, (0,), [line], masked, sums)
    for step in range(1, HALF):
        from_low = lax.ppermute(from_low, ("owner", "rep"), ring_step(1))
        from_high = lax.ppermute(from_high, ("owner", "rep"), ring_step(-1))
        sums = planes_dot(place, (-step, step), [from_low, from_high], masked, sums)
    from_low = lax.ppermute(from_low, ("owner", "rep"), ring_step(1))
    kept, away = planes_dot(place, (HALF,), [from_low], masked, sums)

    arrived = lax.ppermute(away, "rep", [(0, 1), (1, 0)])
    near_a, near_b, own = share(place, kept, arrived)
    axes = ("red", "rep")
    near_a = lax.ppermute(near_a, axes, red_step(1))
    near_b = lax.ppermute(near_b, axes, red_step(1))
    relay = lax.ppermute(added(own[0], near_a[0]), axes, red_step(2))
    back = lax.ppermute(added(own[1], near_a[1]), axes, red_step(-2))
    ahead = lax.ppermute(added(own[2], near_b[0], relay), axes, red_step(2))
    return added(own[3], near_b[1], back, ahead)


def solution(mesh):
    return jax.shard_map(
        per_device,
        mesh=mesh,
        in_specs=(
            P("owner", ("red", "rep")),
            P(("red", "rep"), "owner"),
            P(("red", "rep"), "owner"),
        ),
        out_specs=P(("red", "rep"), "owner"),
        check_vma=False,
    )
```

```python
import functools

import jax
import jax.numpy as jnp
from jax import lax
from jax.experimental import pallas as pl
from jax.experimental.pallas import tpu as pltpu
from jax.sharding import PartitionSpec as P

TILE = 128
SIDE = 8
FAR = 4
CLASSES = 4
ROWS = 16
VMEM = pl.BlockSpec(memory_space=pltpu.VMEM)
SMEM = pl.BlockSpec(memory_space=pltpu.SMEM)
HBM = pl.BlockSpec(memory_space=pltpu.HBM)


def member(z, x, core):
    return (z % SIDE * SIDE + x % SIDE) * 2 + core


def far_groups():
    return [
        [member(pz + 2 * a, px + 2 * b, core) for a in range(FAR) for b in range(FAR)]
        for core in range(2)
        for pz in range(2)
        for px in range(2)
    ]


def near_pairs(dz, dx):
    def partner(place, core):
        return place + 1 if (place + core) % 2 == 0 else place - 1

    return [
        (member(z, x, core), member(partner(z, core) if dz else z, partner(x, core) if dx else x, core))
        for z in range(SIDE)
        for x in range(SIDE)
        for core in range(2)
    ]


def red_step(step):
    return [(y * 2 + c, (y + (step if c == 0 else -step)) % SIDE * 2 + c) for y in range(SIDE) for c in range(2)]


def class_rows(place_ref, rows_ref):
    rep = place_ref[0]
    depth = rows_ref.shape[-1]
    parts = [rows_ref[:, half].reshape(-1, depth) for half in (rep, 1 - rep)]
    return jnp.concatenate(parts, axis=0)


def put(index, here, total, kept_ref, away_ref):
    total = total.astype(kept_ref.dtype).reshape((2,) + kept_ref.shape[1:-1] + (total.shape[-1],))
    kept_ref[index, ..., here] = total[0]
    away_ref[index % away_ref.shape[0], ..., here] = total[1]


def first_kernel(place_ref, bits_hbm, ints_hbm, rows_ref, kept_ref, away_ref, masked_ref, bits_ref, ints_ref, sems):
    cols = ints_ref.shape[1]
    width = 256
    tiles = [slice(start, start + width) for start in range(0, cols, width)]
    bits_copy = pltpu.make_async_copy(bits_hbm, bits_ref, sems.at[len(tiles)])
    bits_copy.start()
    copies = [
        pltpu.make_async_copy(ints_hbm.at[:, here], ints_ref.at[:, here], sems.at[i]) for i, here in enumerate(tiles)
    ]
    for copy in copies:
        copy.start()
    rows = class_rows(place_ref, rows_ref)
    bits_copy.wait()
    for here, copy in zip(tiles, copies):
        copy.wait()
        for q in range(ints_ref.shape[0] // TILE):
            for p in range(here.start // TILE, here.stop // TILE):
                tile = (slice(q * TILE, (q + 1) * TILE), slice(p * TILE, (p + 1) * TILE))
                bit = jnp.broadcast_to(bits_ref[q : q + 1, p : p + 1], (TILE, TILE))
                masked_ref[tile] = ints_ref[tile] * bit.astype(jnp.float32).astype(ints_ref.dtype)
        total = jnp.dot(rows, masked_ref[:, here], preferred_element_type=jnp.float32)
        put(0, here, total, kept_ref, away_ref)


def sums_shape(rows, cols, classes=CLASSES):
    far, _, pairs, _, _ = rows.shape
    return jax.ShapeDtypeStruct((classes, far, pairs, ROWS, cols), jnp.bfloat16)


def first_dot(place, bits, ints, rows):
    depth, cols = ints.shape
    return pl.pallas_call(
        first_kernel,
        in_specs=[SMEM, HBM, HBM, VMEM],
        out_specs=[VMEM, VMEM, VMEM],
        out_shape=[
            sums_shape(rows, cols),
            sums_shape(rows, cols, CLASSES - 1),
            jax.ShapeDtypeStruct(ints.shape, ints.dtype),
        ],
        scratch_shapes=[
            pltpu.VMEM(bits.shape, bits.dtype),
            pltpu.VMEM(ints.shape, ints.dtype),
            pltpu.SemaphoreType.DMA((cols // 256 + 1,)),
        ],
        compiler_params=pltpu.CompilerParams(vmem_limit_bytes=16 * 1024 * 1024),
        cost_estimate=pl.CostEstimate(
            flops=rows.size * cols * 2, bytes_accessed=2 * rows.size + 4 * ints.size, transcendentals=0
        ),
    )(place, bits, ints, rows)


def dot_kernel(index, place_ref, rows_ref, masked_ref, *refs):
    kept_ref, away_ref = refs[-2:]
    width = 256
    rows = class_rows(place_ref, rows_ref)
    for start in range(0, masked_ref.shape[1], width):
        here = slice(start, start + width)
        total = jnp.dot(rows, masked_ref[:, here], preferred_element_type=jnp.float32)
        put(index, here, total, kept_ref, away_ref)


def dot(place, index, rows, masked, *sums):
    cols = masked.shape[1]
    away = sums_shape(rows, cols, CLASSES - 1 if len(sums) == 2 else 1)
    return pl.pallas_call(
        functools.partial(dot_kernel, index),
        in_specs=[SMEM] + [VMEM] * (2 + len(sums)),
        out_specs=[VMEM, VMEM],
        out_shape=[sums_shape(rows, cols), away],
        input_output_aliases={3 + i: i for i in range(len(sums))},
        compiler_params=pltpu.CompilerParams(vmem_limit_bytes=16 * 1024 * 1024),
        cost_estimate=pl.CostEstimate(
            flops=rows.size * cols * 2, bytes_accessed=2 * rows.size + 2 * masked.size, transcendentals=0
        ),
    )(place, rows, masked, *sums)


def share_kernel(steps, place_ref, kept_ref, early_ref, late_ref, *out_refs):
    z, x, y, way = place_ref[1], place_ref[2], place_ref[3], 1 - 2 * place_ref[0]
    flat = [step for group in steps for step in group]
    outs = [(ref, i) for ref, group in zip(out_refs, steps) for i in range(len(group))]
    for step, (out_ref, i) in zip(flat, outs):
        index = (y + way * step + SIDE) & (SIDE - 1)
        dz = (index ^ z) & 1
        a = index >> 1
        for dx in range(2):
            one = kept_ref[2 * dz + dx, a]
            if dx == 0:
                other = early_ref[2 * dz, a]
            else:
                other = jnp.where(dz == 0, early_ref[1, a], late_ref[0, a])
            out_ref[i, :, (x + dx) & 1] = (one.astype(jnp.float32) + other.astype(jnp.float32)).astype(one.dtype)


def share(place, steps, kept, early, late):
    _, _, pairs, rows, cols = kept.shape
    return pl.pallas_call(
        functools.partial(share_kernel, steps),
        in_specs=[SMEM, VMEM, VMEM, VMEM],
        out_specs=[VMEM] * len(steps),
        out_shape=[jax.ShapeDtypeStruct((len(group), pairs, 2, rows, cols), kept.dtype) for group in steps],
        compiler_params=pltpu.CompilerParams(vmem_limit_bytes=16 * 1024 * 1024),
        cost_estimate=pl.CostEstimate(flops=kept.size, bytes_accessed=6 * kept.size, transcendentals=0),
    )(place, kept, early, late)


def added(*terms):
    return sum(t.astype(jnp.float32) for t in terms).astype(jnp.bfloat16)


def per_device(amps, ints, bits):
    owner, y, rep = (lax.axis_index(name).astype(jnp.int32) for name in ("owner", "red", "rep"))
    place = jnp.stack([rep, owner >> 3, owner & (SIDE - 1), y])
    depth = amps.shape[1]
    cols = ints.shape[1]

    copies = jnp.broadcast_to(amps[None], (FAR * FAR,) + amps.shape)
    mine = lax.all_to_all(copies, ("owner", "rep"), 0, 0, axis_index_groups=far_groups(), tiled=True)
    mine = mine.reshape(FAR, 2, 2, ROWS, depth)
    near = [lax.ppermute(mine, ("owner", "rep"), near_pairs(dz, dx)) for dz, dx in ((0, 1), (1, 0), (1, 1))]
    kept, early, masked = first_dot(place, bits, ints, mine)
    kept, early = dot(place, 1, near[0], masked, kept, early)
    kept, early = dot(place, 2, near[1], masked, kept, early)
    swap = [(0, 1), (1, 0)]
    early = lax.ppermute(early, "rep", swap)
    kept, late = dot(place, 3, near[2], masked, kept)
    late = lax.ppermute(late, "rep", swap)

    def along(step, part):
        return lax.ppermute(part, ("red", "rep"), red_step(step))

    groups = ((-1, -4), (1, 3), (-2,), (-3,), (2,), (0,))
    down, up, two_down, three_down, two_up, own = share(place, groups, kept, early, late)
    down, up, two_down = along(-1, down), along(1, up), along(-2, two_down)
    three_down = along(-3, added(three_down[0], down[1]))
    two_up = along(2, added(two_up[0], up[1]))
    return added(own[0], down[0], up[0], two_down[0], three_down, two_up).reshape(-1, cols)


def solution(mesh):
    return jax.shard_map(
        per_device,
        mesh=mesh,
        in_specs=(
            P("owner", ("red", "rep")),
            P(("red", "rep"), "owner"),
            P(("red", "rep"), "owner"),
        ),
        out_specs=P(("red", "rep"), "owner"),
        check_vma=False,
    )
```

```python
import functools

import jax
import jax.numpy as jnp
from jax import lax
from jax.experimental import pallas as pl
from jax.experimental.pallas import tpu as pltpu
from jax.sharding import PartitionSpec as P

TILE = 128
SIDE = 8
FAR = 4
PART = 2
CLASSES = 2 * PART
ROWS = 16
VMEM = pl.BlockSpec(memory_space=pltpu.VMEM)
SMEM = pl.BlockSpec(memory_space=pltpu.SMEM)
HBM = pl.BlockSpec(memory_space=pltpu.HBM)


def member(z, x, core):
    return (z % SIDE * SIDE + x % SIDE) * 2 + core


def far_groups():
    return [
        [member(pz + 2 * a, px + 2 * b, core) for a in range(FAR) for b in range(FAR)]
        for core in range(2)
        for pz in range(2)
        for px in range(2)
    ]


def near_pairs(dz, dx):
    def partner(place, core):
        return place + 1 if (place + core) % 2 == 0 else place - 1

    return [
        (member(z, x, core), member(partner(z, core) if dz else z, partner(x, core) if dx else x, core))
        for z in range(SIDE)
        for x in range(SIDE)
        for core in range(2)
    ]


def red_step(step):
    return [(y * 2 + c, (y + (step if c == 0 else -step)) % SIDE * 2 + c) for y in range(SIDE) for c in range(2)]


def half_rows(half, rows_ref):
    return rows_ref[:, half].reshape(-1, rows_ref.shape[-1])


def put(index, here, total, out_ref):
    out_ref[index, ..., here] = total.astype(out_ref.dtype).reshape(out_ref.shape[1:-1] + (total.shape[-1],))


def class_dot(index, place_ref, rows_ref, masked_ref, tiles, kept_ref, away_ref):
    rep = place_ref[0]
    rows = jnp.concatenate([half_rows(half, rows_ref) for half in (rep, 1 - rep)], axis=0)
    for here in tiles:
        total = jnp.dot(rows, masked_ref[:, here], preferred_element_type=jnp.float32)
        put(index, here, total[: rows.shape[0] // 2], kept_ref)
        put(index, here, total[rows.shape[0] // 2 :], away_ref)


def col_tiles(cols, width=256):
    return [slice(start, start + width) for start in range(0, cols, width)]


def first_kernel(place_ref, bits_hbm, ints_hbm, rows_ref, kept_ref, away_ref, masked_ref, bits_ref, ints_ref, sems):
    tiles = col_tiles(ints_ref.shape[1])
    bits_copy = pltpu.make_async_copy(bits_hbm, bits_ref, sems.at[len(tiles)])
    bits_copy.start()
    copies = [
        pltpu.make_async_copy(ints_hbm.at[:, here], ints_ref.at[:, here], sems.at[i]) for i, here in enumerate(tiles)
    ]
    for copy in copies:
        copy.start()
    bits_copy.wait()
    for here, copy in zip(tiles, copies):
        copy.wait()
        for q in range(ints_ref.shape[0] // TILE):
            for p in range(here.start // TILE, here.stop // TILE):
                tile = (slice(q * TILE, (q + 1) * TILE), slice(p * TILE, (p + 1) * TILE))
                bit = jnp.broadcast_to(bits_ref[q : q + 1, p : p + 1], (TILE, TILE))
                masked_ref[tile] = ints_ref[tile] * bit.astype(jnp.float32).astype(ints_ref.dtype)
        class_dot(0, place_ref, rows_ref, masked_ref, [here], kept_ref, away_ref)


def sums_shape(rows, cols, classes=CLASSES):
    far, _, pairs, _, _ = rows.shape
    return jax.ShapeDtypeStruct((classes, far, pairs, ROWS, cols), jnp.bfloat16)


def first_dot(place, bits, ints, rows):
    depth, cols = ints.shape
    return pl.pallas_call(
        first_kernel,
        in_specs=[SMEM, HBM, HBM, VMEM],
        out_specs=[VMEM, VMEM, VMEM],
        out_shape=[
            sums_shape(rows, cols),
            sums_shape(rows, cols, PART),
            jax.ShapeDtypeStruct(ints.shape, ints.dtype),
        ],
        scratch_shapes=[
            pltpu.VMEM(bits.shape, bits.dtype),
            pltpu.VMEM(ints.shape, ints.dtype),
            pltpu.SemaphoreType.DMA((cols // 256 + 1,)),
        ],
        compiler_params=pltpu.CompilerParams(vmem_limit_bytes=16 * 1024 * 1024),
        cost_estimate=pl.CostEstimate(
            flops=rows.size * cols * 2, bytes_accessed=2 * rows.size + 4 * ints.size, transcendentals=0
        ),
    )(place, bits, ints, rows)


def second_kernel(place_ref, rows_ref, masked_ref, _, __, kept_ref, away_ref):
    class_dot(1, place_ref, rows_ref, masked_ref, col_tiles(masked_ref.shape[1]), kept_ref, away_ref)


def second_dot(place, rows, masked, kept, away):
    cols = masked.shape[1]
    return pl.pallas_call(
        second_kernel,
        in_specs=[SMEM] + [VMEM] * 4,
        out_specs=[VMEM, VMEM],
        out_shape=[sums_shape(rows, cols), sums_shape(rows, cols, PART)],
        input_output_aliases={3: 0, 4: 1},
        compiler_params=pltpu.CompilerParams(vmem_limit_bytes=16 * 1024 * 1024),
        cost_estimate=pl.CostEstimate(
            flops=rows.size * cols * 2, bytes_accessed=2 * rows.size + 2 * masked.size, transcendentals=0
        ),
    )(place, rows, masked, kept, away)


def last_kernel(other, first, place_ref, side_ref, corner_ref, masked_ref, *refs):
    out_ref = refs[-1]
    rep = place_ref[0]
    half = 1 - rep if other else rep
    rows = jnp.concatenate([half_rows(half, ref) for ref in (side_ref, corner_ref)], axis=0)
    for here in col_tiles(masked_ref.shape[1]):
        total = jnp.dot(rows, masked_ref[:, here], preferred_element_type=jnp.float32)
        for i in range(PART):
            put(first + i, here, total[i * rows.shape[0] // PART : (i + 1) * rows.shape[0] // PART], out_ref)


def last_dot(place, other, side, corner, masked, *kept):
    cols = masked.shape[1]
    return pl.pallas_call(
        functools.partial(last_kernel, other, 0 if other else PART),
        in_specs=[SMEM] + [VMEM] * (3 + len(kept)),
        out_specs=VMEM,
        out_shape=sums_shape(side, cols, PART if other else CLASSES),
        input_output_aliases={} if other else {4: 0},
        compiler_params=pltpu.CompilerParams(vmem_limit_bytes=16 * 1024 * 1024),
        cost_estimate=pl.CostEstimate(
            flops=side.size * cols * 2, bytes_accessed=2 * side.size + 2 * masked.size, transcendentals=0
        ),
    )(place, side, corner, masked, *kept)


def share_kernel(steps, place_ref, kept_ref, early_ref, late_ref, *out_refs):
    z, x, y, way = place_ref[1], place_ref[2], place_ref[3], 1 - 2 * place_ref[0]
    flat = [step for group in steps for step in group]
    outs = [(ref, i) for ref, group in zip(out_refs, steps) for i in range(len(group))]
    for step, (out_ref, i) in zip(flat, outs):
        index = (y + way * step + SIDE) & (SIDE - 1)
        dz = (index ^ z) & 1
        a = index >> 1
        for dx in range(2):
            one = kept_ref[2 * dz + dx, a]
            other = jnp.where(dz == 0, early_ref[dx, a], late_ref[dx, a])
            out_ref[i, :, (x + dx) & 1] = (one.astype(jnp.float32) + other.astype(jnp.float32)).astype(one.dtype)


def share(place, steps, kept, early, late):
    _, _, pairs, rows, cols = kept.shape
    return pl.pallas_call(
        functools.partial(share_kernel, steps),
        in_specs=[SMEM, VMEM, VMEM, VMEM],
        out_specs=[VMEM] * len(steps),
        out_shape=[jax.ShapeDtypeStruct((len(group), pairs, 2, rows, cols), kept.dtype) for group in steps],
        compiler_params=pltpu.CompilerParams(vmem_limit_bytes=16 * 1024 * 1024),
        cost_estimate=pl.CostEstimate(flops=kept.size, bytes_accessed=6 * kept.size, transcendentals=0),
    )(place, kept, early, late)


def added(*terms):
    return sum(t.astype(jnp.float32) for t in terms).astype(jnp.bfloat16)


def per_device(amps, ints, bits):
    owner, y, rep = (lax.axis_index(name).astype(jnp.int32) for name in ("owner", "red", "rep"))
    place = jnp.stack([rep, owner >> 3, owner & (SIDE - 1), y])
    depth = amps.shape[1]
    cols = ints.shape[1]

    copies = jnp.broadcast_to(amps[None], (FAR * FAR,) + amps.shape)
    mine = lax.all_to_all(copies, ("owner", "rep"), 0, 0, axis_index_groups=far_groups(), tiled=True)
    mine = mine.reshape(FAR, 2, 2, ROWS, depth)
    near = [lax.ppermute(mine, ("owner", "rep"), near_pairs(dz, dx)) for dz, dx in ((0, 1), (1, 0), (1, 1))]
    swap = [(0, 1), (1, 0)]
    kept, early, masked = first_dot(place, bits, ints, mine)
    kept, early = second_dot(place, near[0], masked, kept, early)
    early = lax.ppermute(early, "rep", swap)
    late = lax.ppermute(last_dot(place, True, near[1], near[2], masked), "rep", swap)
    kept = last_dot(place, False, near[1], near[2], masked, kept)

    def along(step, part):
        return lax.ppermute(part, ("red", "rep"), red_step(step))

    groups = ((-1, -4), (1, 3), (-2,), (-3,), (2,), (0,))
    down, up, two_down, three_down, two_up, own = share(place, groups, kept, early, late)
    down, up, two_down = along(-1, down), along(1, up), along(-2, two_down)
    three_down = along(-3, added(three_down[0], down[1]))
    two_up = along(2, added(two_up[0], up[1]))
    return added(own[0], down[0], up[0], two_down[0], three_down, two_up).reshape(-1, cols)


def solution(mesh):
    return jax.shard_map(
        per_device,
        mesh=mesh,
        in_specs=(
            P("owner", ("red", "rep")),
            P(("red", "rep"), "owner"),
            P(("red", "rep"), "owner"),
        ),
        out_specs=P(("red", "rep"), "owner"),
        check_vma=False,
    )
```

```python
import functools

import jax
import jax.numpy as jnp
from jax import lax
from jax.experimental import pallas as pl
from jax.experimental.pallas import tpu as pltpu
from jax.sharding import PartitionSpec as P

TILE = 128
SIDE = 8
FAR = 4
PART = 2
CLASSES = 2 * PART
ROWS = 16
VMEM = pl.BlockSpec(memory_space=pltpu.VMEM)
SMEM = pl.BlockSpec(memory_space=pltpu.SMEM)


def member(z, x, core):
    return (z % SIDE * SIDE + x % SIDE) * 2 + core


def far_groups():
    return [
        [member(pz + 2 * a, px + 2 * b, core) for a in range(FAR) for b in range(FAR)]
        for core in range(2)
        for pz in range(2)
        for px in range(2)
    ]


def near_pairs(dz, dx):
    def partner(place, core):
        return place + 1 if (place + core) % 2 == 0 else place - 1

    return [
        (member(z, x, core), member(partner(z, core) if dz else z, partner(x, core) if dx else x, core))
        for z in range(SIDE)
        for x in range(SIDE)
        for core in range(2)
    ]


def red_step(step):
    return [(y * 2 + c, (y + (-step if c == 0 else step)) % SIDE * 2 + c) for y in range(SIDE) for c in range(2)]


def half_rows(half, rows_ref):
    return rows_ref[:, half].reshape(-1, rows_ref.shape[-1])


def put(index, here, total, out_ref):
    out_ref[index, ..., here] = total.astype(out_ref.dtype).reshape(out_ref.shape[1:-1] + (total.shape[-1],))


def class_dot(index, place_ref, rows_ref, masked_ref, tiles, kept_ref, away_ref):
    rep = place_ref[0]
    rows = jnp.concatenate([half_rows(half, rows_ref) for half in (rep, 1 - rep)], axis=0)
    for here in tiles:
        total = jnp.dot(rows, masked_ref[:, here], preferred_element_type=jnp.float32)
        put(index, here, total[: rows.shape[0] // 2], kept_ref)
        put(index, here, total[rows.shape[0] // 2 :], away_ref)


def col_tiles(cols, width=256):
    return [slice(start, start + width) for start in range(0, cols, width)]


def first_kernel(place_ref, bits_ref, ints_ref, rows_ref, kept_ref, away_ref, masked_ref):
    for here in col_tiles(ints_ref.shape[1]):
        for q in range(ints_ref.shape[0] // TILE):
            for p in range(here.start // TILE, here.stop // TILE):
                tile = (slice(q * TILE, (q + 1) * TILE), slice(p * TILE, (p + 1) * TILE))
                bit = jnp.broadcast_to(bits_ref[q : q + 1, p : p + 1], (TILE, TILE))
                masked_ref[tile] = ints_ref[tile] * bit.astype(jnp.float32).astype(ints_ref.dtype)
        class_dot(0, place_ref, rows_ref, masked_ref, [here], kept_ref, away_ref)


def sums_shape(rows, cols, classes=CLASSES):
    far, _, pairs, _, _ = rows.shape
    return jax.ShapeDtypeStruct((classes, far, pairs, ROWS, cols), jnp.bfloat16)


def first_dot(place, bits, ints, rows):
    cols = ints.shape[1]
    return pl.pallas_call(
        first_kernel,
        in_specs=[SMEM, VMEM, VMEM, VMEM],
        out_specs=[VMEM, VMEM, VMEM],
        out_shape=[
            sums_shape(rows, cols),
            sums_shape(rows, cols, PART),
            jax.ShapeDtypeStruct(ints.shape, ints.dtype),
        ],
        compiler_params=pltpu.CompilerParams(vmem_limit_bytes=16 * 1024 * 1024),
        cost_estimate=pl.CostEstimate(
            flops=rows.size * cols * 2, bytes_accessed=2 * rows.size + 4 * ints.size, transcendentals=0
        ),
    )(place, bits, ints, rows)


def second_kernel(place_ref, rows_ref, masked_ref, _, __, kept_ref, away_ref):
    class_dot(1, place_ref, rows_ref, masked_ref, col_tiles(masked_ref.shape[1]), kept_ref, away_ref)


def second_dot(place, rows, masked, kept, away):
    cols = masked.shape[1]
    return pl.pallas_call(
        second_kernel,
        in_specs=[SMEM] + [VMEM] * 4,
        out_specs=[VMEM, VMEM],
        out_shape=[sums_shape(rows, cols), sums_shape(rows, cols, PART)],
        input_output_aliases={3: 0, 4: 1},
        compiler_params=pltpu.CompilerParams(vmem_limit_bytes=16 * 1024 * 1024),
        cost_estimate=pl.CostEstimate(
            flops=rows.size * cols * 2, bytes_accessed=2 * rows.size + 2 * masked.size, transcendentals=0
        ),
    )(place, rows, masked, kept, away)


def last_kernel(other, first, place_ref, side_ref, corner_ref, masked_ref, *refs):
    out_ref = refs[-1]
    rep = place_ref[0]
    half = 1 - rep if other else rep
    rows = jnp.concatenate([half_rows(half, ref) for ref in (side_ref, corner_ref)], axis=0)
    for here in col_tiles(masked_ref.shape[1]):
        total = jnp.dot(rows, masked_ref[:, here], preferred_element_type=jnp.float32)
        for i in range(PART):
            put(first + i, here, total[i * rows.shape[0] // PART : (i + 1) * rows.shape[0] // PART], out_ref)


def last_dot(place, other, side, corner, masked, *kept):
    cols = masked.shape[1]
    return pl.pallas_call(
        functools.partial(last_kernel, other, 0 if other else PART),
        in_specs=[SMEM] + [VMEM] * (3 + len(kept)),
        out_specs=VMEM,
        out_shape=sums_shape(side, cols, PART if other else CLASSES),
        input_output_aliases={} if other else {4: 0},
        compiler_params=pltpu.CompilerParams(vmem_limit_bytes=16 * 1024 * 1024),
        cost_estimate=pl.CostEstimate(
            flops=side.size * cols * 2, bytes_accessed=2 * side.size + 2 * masked.size, transcendentals=0
        ),
    )(place, side, corner, masked, *kept)


def share_kernel(steps, place_ref, kept_ref, early_ref, late_ref, *out_refs):
    z, x, y, way = place_ref[1], place_ref[2], place_ref[3], 2 * place_ref[0] - 1
    flat = [step for group in steps for step in group]
    outs = [(ref, i) for ref, group in zip(out_refs, steps) for i in range(len(group))]
    for step, (out_ref, i) in zip(flat, outs):
        index = (y + way * step + SIDE) & (SIDE - 1)
        dz = (index ^ z) & 1
        a = index >> 1
        for dx in range(2):
            one = jnp.where(dz == 0, kept_ref[2 * dx, a], kept_ref[3 - 2 * dx, a])
            other = jnp.where(dz == dx, early_ref[dx, a], late_ref[1 - dx, a])
            out_ref[i, :, (x + dx) & 1] = (one.astype(jnp.float32) + other.astype(jnp.float32)).astype(one.dtype)


def share(place, steps, kept, early, late):
    _, _, pairs, rows, cols = kept.shape
    return pl.pallas_call(
        functools.partial(share_kernel, steps),
        in_specs=[SMEM, VMEM, VMEM, VMEM],
        out_specs=[VMEM] * len(steps),
        out_shape=[jax.ShapeDtypeStruct((len(group), pairs, 2, rows, cols), kept.dtype) for group in steps],
        compiler_params=pltpu.CompilerParams(vmem_limit_bytes=16 * 1024 * 1024),
        cost_estimate=pl.CostEstimate(flops=kept.size, bytes_accessed=6 * kept.size, transcendentals=0),
    )(place, kept, early, late)


def added(*terms):
    return sum(t.astype(jnp.float32) for t in terms).astype(jnp.bfloat16)


def per_device(amps, ints, bits):
    owner, y, rep = (lax.axis_index(name).astype(jnp.int32) for name in ("owner", "red", "rep"))
    place = jnp.stack([rep, owner >> 3, owner & (SIDE - 1), y])
    depth = amps.shape[1]
    cols = ints.shape[1]

    copies = jnp.broadcast_to(amps[None], (FAR * FAR,) + amps.shape)
    mine = lax.all_to_all(copies, ("owner", "rep"), 0, 0, axis_index_groups=far_groups(), tiled=True)
    mine = mine.reshape(FAR, 2, 2, ROWS, depth)
    near = [lax.ppermute(mine, ("owner", "rep"), near_pairs(dz, dx)) for dz, dx in ((1, 1), (0, 1), (1, 0))]
    swap = [(0, 1), (1, 0)]
    kept, early, masked = first_dot(place, bits, ints, mine)
    kept, early = second_dot(place, near[0], masked, kept, early)
    early = lax.ppermute(early, "rep", swap)
    late = lax.ppermute(last_dot(place, True, near[1], near[2], masked), "rep", swap)
    kept = last_dot(place, False, near[1], near[2], masked, kept)

    def along(step, part):
        return lax.ppermute(part, ("red", "rep"), red_step(step))

    groups = ((-1, -4), (1, 3), (-2,), (-3,), (2,), (0,))
    down, up, two_down, three_down, two_up, own = share(place, groups, kept, early, late)
    down, up, two_down = along(-1, down), along(1, up), along(-2, two_down)
    three_down = along(-3, added(three_down[0], down[1]))
    two_up = along(2, added(two_up[0], up[1]))
    return added(own[0], down[0], up[0], two_down[0], three_down, two_up).reshape(-1, cols)


def solution(mesh):
    return jax.shard_map(
        per_device,
        mesh=mesh,
        in_specs=(
            P("owner", ("red", "rep")),
            P(("red", "rep"), "owner"),
            P(("red", "rep"), "owner"),
        ),
        out_specs=P(("red", "rep"), "owner"),
        check_vma=False,
    )
```

```python
import functools

import jax
import jax.numpy as jnp
from jax import lax
from jax.experimental import pallas as pl
from jax.experimental.pallas import tpu as pltpu
from jax.sharding import PartitionSpec as P

TILE = 128
SIDE = 8
FAR = 4
PART = 2
CLASSES = 2 * PART
ROWS = 16
VMEM = pl.BlockSpec(memory_space=pltpu.VMEM)
SMEM = pl.BlockSpec(memory_space=pltpu.SMEM)


def member(z, x, core):
    return (z % SIDE * SIDE + x % SIDE) * 2 + core


def far_groups():
    return [
        [member(pz + 2 * a, px + 2 * b, core) for a in range(FAR) for b in range(FAR)]
        for core in range(2)
        for pz in range(2)
        for px in range(2)
    ]


def near_pairs(dz, dx):
    def partner(place, core):
        return place + 1 if (place + core) % 2 == 0 else place - 1

    return [
        (member(z, x, core), member(partner(z, core) if dz else z, partner(x, core) if dx else x, core))
        for z in range(SIDE)
        for x in range(SIDE)
        for core in range(2)
    ]


def red_step(step):
    return [(y * 2 + c, (y + (-step if c == 0 else step)) % SIDE * 2 + c) for y in range(SIDE) for c in range(2)]


def half_rows(half, rows_ref):
    return rows_ref[:, half].reshape(-1, rows_ref.shape[-1])


def put(index, here, total, out_ref):
    out_ref[index, ..., here] = total.astype(out_ref.dtype).reshape(out_ref.shape[1:-1] + (total.shape[-1],))


def class_dot(index, place_ref, rows_ref, masked_ref, tiles, kept_ref, away_ref):
    rep = place_ref[0]
    rows = jnp.concatenate([half_rows(half, rows_ref) for half in (rep, 1 - rep)], axis=0)
    for here in tiles:
        total = jnp.dot(rows, masked_ref[:, here], preferred_element_type=jnp.float32)
        put(index, here, total[: rows.shape[0] // 2], kept_ref)
        put(index, here, total[rows.shape[0] // 2 :], away_ref)


def col_tiles(cols, width=256):
    return [slice(start, start + width) for start in range(0, cols, width)]


def first_kernel(place_ref, bits_ref, ints_ref, rows_ref, kept_ref, away_ref, masked_ref):
    for here in col_tiles(ints_ref.shape[1]):
        for q in range(ints_ref.shape[0] // TILE):
            for p in range(here.start // TILE, here.stop // TILE):
                tile = (slice(q * TILE, (q + 1) * TILE), slice(p * TILE, (p + 1) * TILE))
                bit = jnp.broadcast_to(bits_ref[q : q + 1, p : p + 1], (TILE, TILE))
                masked_ref[tile] = ints_ref[tile] * bit.astype(jnp.float32).astype(ints_ref.dtype)
        class_dot(0, place_ref, rows_ref, masked_ref, [here], kept_ref, away_ref)


def sums_shape(rows, cols, classes=CLASSES):
    far, _, pairs, _, _ = rows.shape
    return jax.ShapeDtypeStruct((classes, far, pairs, ROWS, cols), jnp.bfloat16)


def first_dot(place, bits, ints, rows):
    cols = ints.shape[1]
    return pl.pallas_call(
        first_kernel,
        in_specs=[SMEM, VMEM, VMEM, VMEM],
        out_specs=[VMEM, VMEM, VMEM],
        out_shape=[
            sums_shape(rows, cols),
            sums_shape(rows, cols, PART),
            jax.ShapeDtypeStruct(ints.shape, ints.dtype),
        ],
        compiler_params=pltpu.CompilerParams(vmem_limit_bytes=16 * 1024 * 1024),
        cost_estimate=pl.CostEstimate(
            flops=rows.size * cols * 2, bytes_accessed=2 * rows.size + 4 * ints.size, transcendentals=0
        ),
    )(place, bits, ints, rows)


def second_kernel(place_ref, rows_ref, masked_ref, _, __, kept_ref, away_ref):
    class_dot(1, place_ref, rows_ref, masked_ref, col_tiles(masked_ref.shape[1]), kept_ref, away_ref)


def second_dot(place, rows, masked, kept, away):
    cols = masked.shape[1]
    return pl.pallas_call(
        second_kernel,
        in_specs=[SMEM] + [VMEM] * 4,
        out_specs=[VMEM, VMEM],
        out_shape=[sums_shape(rows, cols), sums_shape(rows, cols, PART)],
        input_output_aliases={3: 0, 4: 1},
        compiler_params=pltpu.CompilerParams(vmem_limit_bytes=16 * 1024 * 1024),
        cost_estimate=pl.CostEstimate(
            flops=rows.size * cols * 2, bytes_accessed=2 * rows.size + 2 * masked.size, transcendentals=0
        ),
    )(place, rows, masked, kept, away)


def last_kernel(other, first, place_ref, side_ref, corner_ref, masked_ref, *refs):
    out_ref = refs[-1]
    rep = place_ref[0]
    half = 1 - rep if other else rep
    rows = jnp.concatenate([half_rows(half, ref) for ref in (side_ref, corner_ref)], axis=0)
    for here in col_tiles(masked_ref.shape[1]):
        total = jnp.dot(rows, masked_ref[:, here], preferred_element_type=jnp.float32)
        for i in range(PART):
            put(first + i, here, total[i * rows.shape[0] // PART : (i + 1) * rows.shape[0] // PART], out_ref)


def last_dot(place, other, side, corner, masked, *kept):
    cols = masked.shape[1]
    return pl.pallas_call(
        functools.partial(last_kernel, other, 0 if other else PART),
        in_specs=[SMEM] + [VMEM] * (3 + len(kept)),
        out_specs=VMEM,
        out_shape=sums_shape(side, cols, PART if other else CLASSES),
        input_output_aliases={} if other else {4: 0},
        compiler_params=pltpu.CompilerParams(vmem_limit_bytes=16 * 1024 * 1024),
        cost_estimate=pl.CostEstimate(
            flops=side.size * cols * 2, bytes_accessed=2 * side.size + 2 * masked.size, transcendentals=0
        ),
    )(place, side, corner, masked, *kept)


def share_kernel(steps, place_ref, kept_ref, early_ref, late_ref, *out_refs):
    z, x, y, way = place_ref[1], place_ref[2], place_ref[3], 2 * place_ref[0] - 1
    flat = [step for group in steps for step in group]
    outs = [(ref, i) for ref, group in zip(out_refs, steps) for i in range(len(group))]
    for step, (out_ref, i) in zip(flat, outs):
        index = (y + way * step + SIDE) & (SIDE - 1)
        dz = (index ^ z) & 1
        a = index >> 1
        for dx in range(2):
            one = jnp.where(dz == 0, kept_ref[3 * dx, a], kept_ref[2 - dx, a])
            other = jnp.where(dz == dx, early_ref[dx, a], late_ref[dx, a])
            out_ref[i, :, (x + dx) & 1] = (one.astype(jnp.float32) + other.astype(jnp.float32)).astype(one.dtype)


def share(place, steps, kept, early, late):
    _, _, pairs, rows, cols = kept.shape
    return pl.pallas_call(
        functools.partial(share_kernel, steps),
        in_specs=[SMEM, VMEM, VMEM, VMEM],
        out_specs=[VMEM] * len(steps),
        out_shape=[jax.ShapeDtypeStruct((len(group), pairs, 2, rows, cols), kept.dtype) for group in steps],
        compiler_params=pltpu.CompilerParams(vmem_limit_bytes=16 * 1024 * 1024),
        cost_estimate=pl.CostEstimate(flops=kept.size, bytes_accessed=6 * kept.size, transcendentals=0),
    )(place, kept, early, late)


def added(*terms):
    return sum(t.astype(jnp.float32) for t in terms).astype(jnp.bfloat16)


def per_device(amps, ints, bits):
    owner, y, rep = (lax.axis_index(name).astype(jnp.int32) for name in ("owner", "red", "rep"))
    place = jnp.stack([rep, owner >> 3, owner & (SIDE - 1), y])
    depth = amps.shape[1]
    cols = ints.shape[1]

    copies = jnp.broadcast_to(amps[None], (FAR * FAR,) + amps.shape)
    mine = lax.all_to_all(copies, ("owner", "rep"), 0, 0, axis_index_groups=far_groups(), tiled=True)
    mine = mine.reshape(FAR, 2, 2, ROWS, depth)
    near = [lax.ppermute(mine, ("owner", "rep"), near_pairs(dz, dx)) for dz, dx in ((1, 1), (1, 0), (0, 1))]
    swap = [(0, 1), (1, 0)]
    kept, early, masked = first_dot(place, bits, ints, mine)
    kept, early = second_dot(place, near[0], masked, kept, early)
    early = lax.ppermute(early, "rep", swap)
    late = lax.ppermute(last_dot(place, True, near[1], near[2], masked), "rep", swap)
    kept = last_dot(place, False, near[1], near[2], masked, kept)

    def along(step, part):
        return lax.ppermute(part, ("red", "rep"), red_step(step))

    groups = ((-1, -4), (1, 3), (-2,), (-3,), (2,), (0,))
    down, up, two_down, three_down, two_up, own = share(place, groups, kept, early, late)
    down, up, two_down = along(-1, down), along(1, up), along(-2, two_down)
    three_down = along(-3, added(three_down[0], down[1]))
    two_up = along(2, added(two_up[0], up[1]))
    return added(own[0], down[0], up[0], two_down[0], three_down, two_up).reshape(-1, cols)


def solution(mesh):
    return jax.shard_map(
        per_device,
        mesh=mesh,
        in_specs=(
            P("owner", ("red", "rep")),
            P(("red", "rep"), "owner"),
            P(("red", "rep"), "owner"),
        ),
        out_specs=P(("red", "rep"), "owner"),
        check_vma=False,
    )
```

```python
import functools

import jax
import jax.numpy as jnp
from jax import lax
from jax.experimental import pallas as pl
from jax.experimental.pallas import tpu as pltpu
from jax.sharding import PartitionSpec as P

TILE = 128
SIDE = 8
FAR = 4
PART = 2
ROWS = 16
VMEM = pl.BlockSpec(memory_space=pltpu.VMEM)
SMEM = pl.BlockSpec(memory_space=pltpu.SMEM)


def member(z, x, core):
    return (z % SIDE * SIDE + x % SIDE) * 2 + core


def far_groups():
    return [
        [member(pz + 2 * a, px + 2 * b, core) for a in range(FAR) for b in range(FAR)]
        for core in range(2)
        for pz in range(2)
        for px in range(2)
    ]


def near_pairs(dz, dx):
    def partner(place, core):
        return place + 1 if (place + core) % 2 == 0 else place - 1

    return [
        (member(z, x, core), member(partner(z, core) if dz else z, partner(x, core) if dx else x, core))
        for z in range(SIDE)
        for x in range(SIDE)
        for core in range(2)
    ]


def red_step(step):
    return [(y * 2 + c, (y + (-step if c == 0 else step)) % SIDE * 2 + c) for y in range(SIDE) for c in range(2)]


def half_rows(half, rows_ref):
    return rows_ref[:, half].reshape(-1, rows_ref.shape[-1])


def put(index, here, total, out_ref):
    out_ref[index, ..., here] = total.astype(out_ref.dtype).reshape(out_ref.shape[1:-1] + (total.shape[-1],))


def class_dot(index, place_ref, rows_ref, masked_ref, tiles, kept_ref, away_ref):
    rep = place_ref[0]
    rows = jnp.concatenate([half_rows(half, rows_ref) for half in (rep, 1 - rep)], axis=0)
    for here in tiles:
        total = jnp.dot(rows, masked_ref[:, here], preferred_element_type=jnp.float32)
        put(index, here, total[: rows.shape[0] // 2], kept_ref)
        put(index, here, total[rows.shape[0] // 2 :], away_ref)


def col_tiles(cols, width=256):
    return [slice(start, start + width) for start in range(0, cols, width)]


def first_kernel(place_ref, bits_ref, ints_ref, rows_ref, kept_ref, away_ref, masked_ref):
    for here in col_tiles(ints_ref.shape[1]):
        for q in range(ints_ref.shape[0] // TILE):
            for p in range(here.start // TILE, here.stop // TILE):
                tile = (slice(q * TILE, (q + 1) * TILE), slice(p * TILE, (p + 1) * TILE))
                bit = jnp.broadcast_to(bits_ref[q : q + 1, p : p + 1], (TILE, TILE))
                masked_ref[tile] = ints_ref[tile] * bit.astype(jnp.float32).astype(ints_ref.dtype)
        class_dot(0, place_ref, rows_ref, masked_ref, [here], kept_ref, away_ref)


def sums_shape(rows, cols):
    far, _, pairs, _, _ = rows.shape
    return jax.ShapeDtypeStruct((PART, far, pairs, ROWS, cols), jnp.bfloat16)


def first_dot(place, bits, ints, rows):
    cols = ints.shape[1]
    return pl.pallas_call(
        first_kernel,
        in_specs=[SMEM, VMEM, VMEM, VMEM],
        out_specs=[VMEM, VMEM, VMEM],
        out_shape=[
            sums_shape(rows, cols),
            sums_shape(rows, cols),
            jax.ShapeDtypeStruct(ints.shape, ints.dtype),
        ],
        compiler_params=pltpu.CompilerParams(vmem_limit_bytes=16 * 1024 * 1024),
        cost_estimate=pl.CostEstimate(
            flops=rows.size * cols * 2, bytes_accessed=2 * rows.size + 4 * ints.size, transcendentals=0
        ),
    )(place, bits, ints, rows)


def second_kernel(place_ref, rows_ref, masked_ref, _, __, kept_ref, away_ref):
    class_dot(1, place_ref, rows_ref, masked_ref, col_tiles(masked_ref.shape[1]), kept_ref, away_ref)


def second_dot(place, rows, masked, kept, away):
    cols = masked.shape[1]
    return pl.pallas_call(
        second_kernel,
        in_specs=[SMEM] + [VMEM] * 4,
        out_specs=[VMEM, VMEM],
        out_shape=[sums_shape(rows, cols), sums_shape(rows, cols)],
        input_output_aliases={3: 0, 4: 1},
        compiler_params=pltpu.CompilerParams(vmem_limit_bytes=16 * 1024 * 1024),
        cost_estimate=pl.CostEstimate(
            flops=rows.size * cols * 2, bytes_accessed=2 * rows.size + 2 * masked.size, transcendentals=0
        ),
    )(place, rows, masked, kept, away)


def late_dots(half, side_ref, corner_ref, masked_ref, out_ref):
    rows = jnp.concatenate([half_rows(half, ref) for ref in (side_ref, corner_ref)], axis=0)
    for here in col_tiles(masked_ref.shape[1]):
        total = jnp.dot(rows, masked_ref[:, here], preferred_element_type=jnp.float32)
        for i in range(PART):
            put(i, here, total[i * rows.shape[0] // PART : (i + 1) * rows.shape[0] // PART], out_ref)


def away_kernel(place_ref, side_ref, corner_ref, masked_ref, out_ref):
    late_dots(1 - place_ref[0], side_ref, corner_ref, masked_ref, out_ref)


def away_dot(place, side, corner, masked):
    cols = masked.shape[1]
    return pl.pallas_call(
        away_kernel,
        in_specs=[SMEM] + [VMEM] * 3,
        out_specs=VMEM,
        out_shape=sums_shape(side, cols),
        compiler_params=pltpu.CompilerParams(vmem_limit_bytes=16 * 1024 * 1024),
        cost_estimate=pl.CostEstimate(
            flops=side.size * cols * 2, bytes_accessed=2 * side.size + 2 * masked.size, transcendentals=0
        ),
    )(place, side, corner, masked)


def share(late, steps, place_ref, kept_ref, arrived_ref, out_refs):
    z, x, y, way = place_ref[1], place_ref[2], place_ref[3], 2 * place_ref[0] - 1
    for group, out_ref in zip(steps, out_refs):
        for i, step in enumerate(group):
            index = (y + way * step + SIDE) & (SIDE - 1)
            dz = (index ^ z) & 1
            which = 1 - dz if late else dz
            one, other = kept_ref[which, index >> 1], arrived_ref[which, index >> 1]
            px = (x + which) & 1
            out_ref[i, :, px] = (one.astype(jnp.float32) + other.astype(jnp.float32)).astype(one.dtype)


def kept_kernel(steps, place_ref, side_ref, corner_ref, masked_ref, early_ref, arrived_ref, kept_ref, *out_refs):
    late_dots(place_ref[0], side_ref, corner_ref, masked_ref, kept_ref)
    share(False, steps, place_ref, early_ref, arrived_ref, out_refs)


def kept_dot(place, steps, side, corner, masked, early, arrived):
    cols = masked.shape[1]
    _, _, pairs, rows, _ = early.shape
    return pl.pallas_call(
        functools.partial(kept_kernel, steps),
        in_specs=[SMEM] + [VMEM] * 5,
        out_specs=[VMEM] * (1 + len(steps)),
        out_shape=[sums_shape(side, cols)]
        + [jax.ShapeDtypeStruct((len(group), pairs, 2, rows, cols), early.dtype) for group in steps],
        compiler_params=pltpu.CompilerParams(vmem_limit_bytes=16 * 1024 * 1024),
        cost_estimate=pl.CostEstimate(
            flops=side.size * cols * 2, bytes_accessed=2 * side.size + 2 * masked.size, transcendentals=0
        ),
    )(place, side, corner, masked, early, arrived)


def late_kernel(steps, place_ref, kept_ref, arrived_ref, *refs):
    share(True, steps, place_ref, kept_ref, arrived_ref, refs[len(steps) :])


def late_share(place, steps, kept, arrived, parts):
    return pl.pallas_call(
        functools.partial(late_kernel, steps),
        in_specs=[SMEM] + [VMEM] * (2 + len(parts)),
        out_specs=[VMEM] * len(parts),
        out_shape=[jax.ShapeDtypeStruct(part.shape, part.dtype) for part in parts],
        input_output_aliases={3 + i: i for i in range(len(parts))},
        compiler_params=pltpu.CompilerParams(vmem_limit_bytes=16 * 1024 * 1024),
        cost_estimate=pl.CostEstimate(flops=kept.size, bytes_accessed=6 * kept.size, transcendentals=0),
    )(place, kept, arrived, *parts)


def added(*terms):
    return sum(t.astype(jnp.float32) for t in terms).astype(jnp.bfloat16)


def per_device(amps, ints, bits):
    owner, y, rep = (lax.axis_index(name).astype(jnp.int32) for name in ("owner", "red", "rep"))
    place = jnp.stack([rep, owner >> 3, owner & (SIDE - 1), y])
    depth = amps.shape[1]
    cols = ints.shape[1]

    copies = jnp.broadcast_to(amps[None], (FAR * FAR,) + amps.shape)
    mine = lax.all_to_all(copies, ("owner", "rep"), 0, 0, axis_index_groups=far_groups(), tiled=True)
    mine = mine.reshape(FAR, 2, 2, ROWS, depth)
    near = [lax.ppermute(mine, ("owner", "rep"), near_pairs(dz, dx)) for dz, dx in ((1, 1), (1, 0), (0, 1))]
    swap = [(0, 1), (1, 0)]
    kept, early, masked = first_dot(place, bits, ints, mine)
    kept, early = second_dot(place, near[0], masked, kept, early)
    early = lax.ppermute(early, "rep", swap)
    late = lax.ppermute(away_dot(place, near[1], near[2], masked), "rep", swap)
    groups = ((-1, -4), (1, 3), (-2,), (-3,), (2,), (0,))
    late_kept, *parts = kept_dot(place, groups, near[1], near[2], masked, kept, early)
    down, up, two_down, three_down, two_up, own = late_share(place, groups, late_kept, late, parts)

    def along(step, part):
        return lax.ppermute(part, ("red", "rep"), red_step(step))

    down, up, two_down = along(-1, down), along(1, up), along(-2, two_down)
    three_down = along(-3, added(three_down[0], down[1]))
    two_up = along(2, added(two_up[0], up[1]))
    return added(own[0], down[0], up[0], two_down[0], three_down, two_up).reshape(-1, cols)


def solution(mesh):
    return jax.shard_map(
        per_device,
        mesh=mesh,
        in_specs=(
            P("owner", ("red", "rep")),
            P(("red", "rep"), "owner"),
            P(("red", "rep"), "owner"),
        ),
        out_specs=P(("red", "rep"), "owner"),
        check_vma=False,
    )
```

```python
import functools

import jax
import jax.numpy as jnp
from jax import lax
from jax.experimental import pallas as pl
from jax.experimental.pallas import tpu as pltpu
from jax.sharding import PartitionSpec as P

TILE = 128
SIDE = 8
FAR = 4
PART = 2
ROWS = 16
VMEM = pl.BlockSpec(memory_space=pltpu.VMEM)
SMEM = pl.BlockSpec(memory_space=pltpu.SMEM)


def member(z, x, core):
    return (z % SIDE * SIDE + x % SIDE) * 2 + core


def far_groups():
    return [
        [member(pz + 2 * a, px + 2 * b, core) for a in range(FAR) for b in range(FAR)]
        for core in range(2)
        for pz in range(2)
        for px in range(2)
    ]


def near_pairs(dz, dx):
    def partner(place, core):
        return place + 1 if (place + core) % 2 == 0 else place - 1

    return [
        (member(z, x, core), member(partner(z, core) if dz else z, partner(x, core) if dx else x, core))
        for z in range(SIDE)
        for x in range(SIDE)
        for core in range(2)
    ]


def red_step(step):
    return [(y * 2 + c, (y + (-step if c == 0 else step)) % SIDE * 2 + c) for y in range(SIDE) for c in range(2)]


def half_rows(half, rows_ref):
    return rows_ref[:, half].reshape(-1, rows_ref.shape[-1])


def put(index, here, total, out_ref):
    out_ref[index, ..., here] = total.astype(out_ref.dtype).reshape(out_ref.shape[1:-1] + (total.shape[-1],))


def class_dot(index, place_ref, rows_ref, masked_ref, tiles, kept_ref, away_ref):
    rep = place_ref[0]
    rows = jnp.concatenate([half_rows(half, rows_ref) for half in (rep, 1 - rep)], axis=0)
    for here in tiles:
        total = jnp.dot(rows, masked_ref[:, here], preferred_element_type=jnp.float32)
        put(index, here, total[: rows.shape[0] // 2], kept_ref)
        put(index, here, total[rows.shape[0] // 2 :], away_ref)


def col_tiles(cols, width=256):
    return [slice(start, start + width) for start in range(0, cols, width)]


def first_kernel(place_ref, bits_ref, ints_ref, rows_ref, kept_ref, away_ref, masked_ref):
    for here in col_tiles(ints_ref.shape[1]):
        for q in range(ints_ref.shape[0] // TILE):
            for p in range(here.start // TILE, here.stop // TILE):
                tile = (slice(q * TILE, (q + 1) * TILE), slice(p * TILE, (p + 1) * TILE))
                bit = jnp.broadcast_to(bits_ref[q : q + 1, p : p + 1], (TILE, TILE))
                masked_ref[tile] = ints_ref[tile] * bit.astype(jnp.float32).astype(ints_ref.dtype)
        class_dot(0, place_ref, rows_ref, masked_ref, [here], kept_ref, away_ref)


def sums_shape(rows, cols):
    far, _, pairs, _, _ = rows.shape
    return jax.ShapeDtypeStruct((PART, far, pairs, ROWS, cols), jnp.bfloat16)


def first_dot(place, bits, ints, rows):
    cols = ints.shape[1]
    return pl.pallas_call(
        first_kernel,
        in_specs=[SMEM, VMEM, VMEM, VMEM],
        out_specs=[VMEM, VMEM, VMEM],
        out_shape=[
            sums_shape(rows, cols),
            sums_shape(rows, cols),
            jax.ShapeDtypeStruct(ints.shape, ints.dtype),
        ],
        compiler_params=pltpu.CompilerParams(vmem_limit_bytes=16 * 1024 * 1024),
        cost_estimate=pl.CostEstimate(
            flops=rows.size * cols * 2, bytes_accessed=2 * rows.size + 4 * ints.size, transcendentals=0
        ),
    )(place, bits, ints, rows)


def second_kernel(place_ref, rows_ref, masked_ref, _, __, kept_ref, away_ref):
    class_dot(1, place_ref, rows_ref, masked_ref, col_tiles(masked_ref.shape[1]), kept_ref, away_ref)


def second_dot(place, rows, masked, kept, away):
    cols = masked.shape[1]
    return pl.pallas_call(
        second_kernel,
        in_specs=[SMEM] + [VMEM] * 4,
        out_specs=[VMEM, VMEM],
        out_shape=[sums_shape(rows, cols), sums_shape(rows, cols)],
        input_output_aliases={3: 0, 4: 1},
        compiler_params=pltpu.CompilerParams(vmem_limit_bytes=16 * 1024 * 1024),
        cost_estimate=pl.CostEstimate(
            flops=rows.size * cols * 2, bytes_accessed=2 * rows.size + 2 * masked.size, transcendentals=0
        ),
    )(place, rows, masked, kept, away)


def late_dots(half, side_ref, corner_ref, masked_ref, out_ref):
    rows = jnp.concatenate([half_rows(half, ref) for ref in (side_ref, corner_ref)], axis=0)
    for here in col_tiles(masked_ref.shape[1]):
        total = jnp.dot(rows, masked_ref[:, here], preferred_element_type=jnp.float32)
        for i in range(PART):
            put(i, here, total[i * rows.shape[0] // PART : (i + 1) * rows.shape[0] // PART], out_ref)


def away_kernel(place_ref, side_ref, corner_ref, masked_ref, out_ref):
    late_dots(1 - place_ref[0], side_ref, corner_ref, masked_ref, out_ref)


def away_dot(place, side, corner, masked):
    cols = masked.shape[1]
    return pl.pallas_call(
        away_kernel,
        in_specs=[SMEM] + [VMEM] * 3,
        out_specs=VMEM,
        out_shape=sums_shape(side, cols),
        compiler_params=pltpu.CompilerParams(vmem_limit_bytes=16 * 1024 * 1024),
        cost_estimate=pl.CostEstimate(
            flops=side.size * cols * 2, bytes_accessed=2 * side.size + 2 * masked.size, transcendentals=0
        ),
    )(place, side, corner, masked)


def share(late, steps, place_ref, kept_ref, arrived_ref, out_refs):
    z, x, y, way = place_ref[1], place_ref[2], place_ref[3], 2 * place_ref[0] - 1
    for group, out_ref in zip(steps, out_refs):
        for i, step in enumerate(group):
            index = (y + way * step + SIDE) & (SIDE - 1)
            dz = (index ^ z) & 1
            which = 1 - dz if late else dz
            one, other = kept_ref[which, index >> 1], arrived_ref[which, index >> 1]
            px = (x + which) & 1
            out_ref[i, :, px] = (one.astype(jnp.float32) + other.astype(jnp.float32)).astype(one.dtype)


def kept_kernel(steps, place_ref, side_ref, corner_ref, masked_ref, early_ref, arrived_ref, kept_ref, *out_refs):
    late_dots(place_ref[0], side_ref, corner_ref, masked_ref, kept_ref)
    share(False, steps, place_ref, early_ref, arrived_ref, out_refs)


def kept_dot(place, steps, side, corner, masked, early, arrived):
    cols = masked.shape[1]
    _, _, pairs, rows, _ = early.shape
    return pl.pallas_call(
        functools.partial(kept_kernel, steps),
        in_specs=[SMEM] + [VMEM] * 5,
        out_specs=[VMEM] * (1 + len(steps)),
        out_shape=[sums_shape(side, cols)]
        + [jax.ShapeDtypeStruct((len(group), pairs, 2, rows, cols), early.dtype) for group in steps],
        compiler_params=pltpu.CompilerParams(vmem_limit_bytes=16 * 1024 * 1024),
        cost_estimate=pl.CostEstimate(
            flops=side.size * cols * 2, bytes_accessed=2 * side.size + 2 * masked.size, transcendentals=0
        ),
    )(place, side, corner, masked, early, arrived)


def late_kernel(steps, place_ref, kept_ref, arrived_ref, *refs):
    share(True, steps, place_ref, kept_ref, arrived_ref, refs[len(steps) :])


def late_share(place, steps, kept, arrived, parts):
    return pl.pallas_call(
        functools.partial(late_kernel, steps),
        in_specs=[SMEM] + [VMEM] * (2 + len(parts)),
        out_specs=[VMEM] * len(parts),
        out_shape=[jax.ShapeDtypeStruct(part.shape, part.dtype) for part in parts],
        input_output_aliases={3 + i: i for i in range(len(parts))},
        compiler_params=pltpu.CompilerParams(vmem_limit_bytes=16 * 1024 * 1024),
        cost_estimate=pl.CostEstimate(flops=kept.size, bytes_accessed=6 * kept.size, transcendentals=0),
    )(place, kept, arrived, *parts)


def added(*terms):
    return sum(t.astype(jnp.float32) for t in terms).astype(jnp.bfloat16)


def per_device(amps, ints, bits):
    owner, y, rep = (lax.axis_index(name).astype(jnp.int32) for name in ("owner", "red", "rep"))
    place = jnp.stack([rep, owner >> 3, owner & (SIDE - 1), y])
    depth = amps.shape[1]
    cols = ints.shape[1]

    copies = jnp.broadcast_to(amps[None], (FAR * FAR,) + amps.shape)
    mine = lax.all_to_all(copies, ("owner", "rep"), 0, 0, axis_index_groups=far_groups(), tiled=True)
    mine = mine.reshape(FAR, 2, 2, ROWS, depth)
    near = [lax.ppermute(mine, ("owner", "rep"), near_pairs(dz, dx)) for dz, dx in ((1, 1), (1, 0), (0, 1))]
    swap = [(0, 1), (1, 0)]
    kept, early, masked = first_dot(place, bits, ints, mine)
    kept, early = second_dot(place, near[0], masked, kept, early)
    early = lax.ppermute(early, "rep", swap)
    late = lax.ppermute(away_dot(place, near[1], near[2], masked), "rep", swap)
    groups = ((1, 3), (-1, -4), (-2,), (2,), (-3,), (0,))
    late_kept, *parts = kept_dot(place, groups, near[1], near[2], masked, kept, early)
    up, down, two_down, two_up, three_down, own = late_share(place, groups, late_kept, late, parts)

    def along(step, part):
        return lax.ppermute(part, ("red", "rep"), red_step(step))

    up, down, two_down = along(1, up), along(-1, down), along(-2, two_down)
    two_up = along(2, added(two_up[0], up[1]))
    three_down = along(-3, added(three_down[0], down[1]))
    return added(own[0], down[0], up[0], two_down[0], three_down, two_up).reshape(-1, cols)


def solution(mesh):
    return jax.shard_map(
        per_device,
        mesh=mesh,
        in_specs=(
            P("owner", ("red", "rep")),
            P(("red", "rep"), "owner"),
            P(("red", "rep"), "owner"),
        ),
        out_specs=P(("red", "rep"), "owner"),
        check_vma=False,
    )
```
